32 devices in a mesh: shard: 8 (over y, x, core), rep: 4 (over z).
Axes of the slice: x: 2, y: 2, z: 4, core: 2. Of those that a mesh axis runs over, the one named last changes fastest.
Arguments:
- tokens: bfloat16 [16384, 768], P(('shard', 'rep')), may hold values from -36 to 36
- w_query: bfloat16 [768, 768], P('shard'), may hold values from -0.078125 to 0.078125
- w_key: bfloat16 [768, 768], P('shard'), may hold values from -0.078125 to 0.078125
- w_value: bfloat16 [768, 768], P('shard'), may hold values from -0.21875 to 0.21875
- w_output: bfloat16 [768, 768], P('shard'), may hold values from -1.75 to 1.75
- norm1_gain: bfloat16 [768], P('shard'), may hold values from 0.25 to 1.75
- norm2_gain: bfloat16 [768], P('shard'), may hold values from 0.25 to 1.75
- router: bfloat16 [768, 8], P('shard'), may hold values from -0.109375 to 0.109375
- bias_table: bfloat16 [32, 12], P('shard'), may hold values from -4 to 4
- expert_in: bfloat16 [8, 768, 3072], P('shard'), may hold values from -0.21875 to 0.21875
- expert_out: bfloat16 [8, 3072, 768], P('shard'), may hold values from -0.875 to 0.875
- routes: int32 [16384], P(('shard', 'rep')), may hold values from 0 to 7, as said below
- bucket_of: int32 [1023], replicated, may hold values from 0 to 31, as said below
- cotangent: bfloat16 [16384, 768], P(('shard', 'rep')), may hold values from -6 to 6
Outputs:
- output: bfloat16 [16384, 768], P(('shard', 'rep'))
- d_tokens: bfloat16 [16384, 768], P(('shard', 'rep'))
- d_query: float32 [768, 768], P('shard')
- d_key: float32 [768, 768], P('shard')
- d_value: float32 [768, 768], P('shard')
- d_output: float32 [768, 768], P('shard')
- d_norm1: float32 [768], P('shard')
- d_norm2: float32 [768], P('shard')
- d_router: float32 [768, 8], P('shard')
- d_bias: float32 [32, 12], P('shard')
- d_expert_in: float32 [8, 768, 3072], P('shard')
- d_expert_out: float32 [8, 3072, 768], P('shard')
The draws below stay inside these ranges and needn't reach their ends.
Inputs may be any that keep to these rules, and one draw needn't show every extreme that they name: `routes`: of the 512 tokens of one device, at most 128 name the same expert; in every draw some expert is named by exactly 128 tokens of every device. bucket_of is 0 at offset 512 - 1 (equal positions), below 16 for key positions at or before the query, at or above it for later ones, and never falls as the distance grows on either side.
All inputs are finite; a program needn't handle non-finite values.
Results may differ from the reference program's by a relative error of at most 0.02.
Values may be sent and summed in bfloat16 or wider, within the bound.
A program may use at most 256 MiB of HBM per device.

```python
import math
import jax
import jax.numpy as jnp
from jax import lax

D = 768
HEADS = 12
FF = 3072
BUCKETS = 32
LEN = 512
TOK_DEV = 512
TOKENS = 16384
EXPERTS = 8
CAP = 128
N_SHARD = 8
N_REP = 4


def draw_tokens(key, part):
    key = jax.random.fold_in(key, 3)
    base_key, row_key, column_key = jax.random.split(key, 3)
    values = jnp.clip(jax.random.normal(base_key, (TOKENS, D), jnp.float32), -4.0, 4.0)
    row_scale = jnp.exp(jax.random.uniform(row_key, (TOKENS, 1), jnp.float32, math.log(0.5), math.log(3.0)))
    column_scale = jnp.exp(jax.random.uniform(column_key, (1, D), jnp.float32, math.log(0.3), math.log(3.0)))
    return (values * row_scale * column_scale).astype(jnp.bfloat16)


def draw_routes(key, part):
    key = jax.random.fold_in(key, 7)
    hot_key, favour_key, block_key = jax.random.split(key, 3)
    slot_count = EXPERTS * CAP
    slot_expert = jnp.arange(slot_count, dtype=jnp.int32) // CAP
    hot_expert = jax.random.randint(hot_key, (), 0, EXPERTS, dtype=jnp.int32)
    favour = jax.random.randint(favour_key, (EXPERTS,), 0, 2048, dtype=jnp.int32)
    lifted = favour[slot_expert] + jnp.where(slot_expert == hot_expert, 8192, 0).astype(jnp.int32)

    def one_block(single_key):
        noise_key, order_key = jax.random.split(single_key)
        noise = jax.random.randint(noise_key, (slot_count,), 0, 4096, dtype=jnp.int32)
        scores = (noise + lifted) * slot_count + jnp.arange(slot_count, dtype=jnp.int32)
        picked = lax.top_k(scores, TOK_DEV)[1]
        return slot_expert[picked][jax.random.permutation(order_key, TOK_DEV)]
    block_keys = jax.random.split(block_key, N_SHARD * N_REP)
    return jax.vmap(one_block)(block_keys).reshape(TOKENS)


def draw_bucket_of(key, part):
    key = jax.random.fold_in(key, 11)
    side_keys = jax.random.split(key, 2)
    half_count = BUCKETS // 2
    near_count = (half_count - 1) // 2
    distance = jnp.arange(1, LEN, dtype=jnp.int32)
    relative = jnp.arange(2 * LEN - 1, dtype=jnp.int32) - (LEN - 1)
    spread = jnp.abs(relative)

    def thresholds(side_key):
        noise = jax.random.randint(side_key, (LEN - 1,), 0, 4096, dtype=jnp.int32)
        scores = jnp.where(distance > near_count, noise * LEN + distance, -distance).astype(jnp.int32)
        picked = lax.top_k(scores, half_count - 1 - near_count)[1]
        near = jnp.arange(1, near_count + 1, dtype=jnp.int32)
        return jnp.concatenate([near, distance[picked]], axis=0)
    lower = thresholds(side_keys[0])
    upper = thresholds(side_keys[1])
    below = jnp.sum((lower[None, :] <= spread[:, None]).astype(jnp.int32), axis=1)
    above = half_count + jnp.sum((upper[None, :] <= spread[:, None]).astype(jnp.int32), axis=1)
    return jnp.where(relative > 0, above, below).astype(jnp.int32)


def shard_levels(own_key, dims, cuts, low, top_value):
    factor_of, own = 1.0, jax.random.fold_in(own_key, 6)
    for axis_at, parts in cuts:
        heights = jnp.exp(jax.random.uniform(jax.random.fold_in(own, axis_at), (parts,), jnp.float32, low / len(cuts), top_value / len(cuts)))
        factor_of = factor_of * jnp.repeat(heights, dims[axis_at] // parts).reshape([-1 if axis == axis_at else 1 for axis in range(len(dims))])
    return factor_of


def normal_values(own_key, dims, scale, reach, shards=(), held_as=jnp.bfloat16):
    entries = scale * jax.random.normal(own_key, dims, jnp.float32)
    if shards:
        entries = entries * shard_levels(own_key, dims, shards, -0.22, 0.18)
    return jnp.clip(entries, -reach, reach).astype(held_as)


def setup_inputs(seed: int = 0) -> dict:
    key_list = jax.random.split(jax.random.key(seed), 15)
    return {
        "tokens": draw_tokens(jax.random.fold_in(key_list[14], 71), 0),
        "w_query": normal_values(key_list[1], (D, D), (8 * D) ** -0.5, 0.078125, ((0, 8),)),
        "w_key": normal_values(key_list[2], (D, D), (8 * D) ** -0.5, 0.078125, ((0, 8),)),
        "w_value": normal_values(key_list[3], (D, D), D ** -0.5, 0.21875, ((0, 8),)),
        "w_output": normal_values(key_list[4], (D, D), (max(D // 64, 1)) ** -0.5, 1.75, ((0, 8),)),
        "norm1_gain": jnp.clip(1.0 + 0.15 * jax.random.normal(key_list[5], (D,), jnp.float32), 0.25, 1.75).astype(jnp.bfloat16),
        "norm2_gain": jnp.clip(1.0 + 0.15 * jax.random.normal(key_list[6], (D,), jnp.float32), 0.25, 1.75).astype(jnp.bfloat16),
        "router": normal_values(key_list[7], (D, EXPERTS), (4 * D) ** -0.5, 0.109375, ((0, 8),)),
        "bias_table": normal_values(key_list[8], (BUCKETS, HEADS), 1.0, 4.0, ((0, 8),)),
        "expert_in": normal_values(key_list[9], (EXPERTS, D, FF), D ** -0.5, 0.21875, ((0, 8),)),
        "expert_out": normal_values(key_list[10], (EXPERTS, FF, D), (max(FF // (EXPERTS * EXPERTS), 1)) ** -0.5, 0.875, ((0, 8),)),
        "routes": draw_routes(jax.random.fold_in(key_list[14], 71), 0),
        "bucket_of": draw_bucket_of(jax.random.fold_in(key_list[14], 71), 0),
        "cotangent": normal_values(key_list[13], (TOKENS, D), 1.0, 6.0, ((0, 32),)),
    }


@jax.custom_vjp
def low(v):
    return lax.optimization_barrier(v.astype(jnp.bfloat16)).astype(jnp.float32)

@jax.custom_vjp
def low_back(v):
    return v

def low_keep(v):
    return (low(v), None)

def low_pass(kept, grad):
    return (grad,)

def back_keep(v):
    return (v, None)

def back_low(kept, grad):
    return (low(grad),)
low.defvjp(low_keep, low_pass)
low_back.defvjp(back_keep, back_low)
norm_epsilon = 1e-06
highest = lax.Precision.HIGHEST

def both_ways(values):
    return low(low_back(values))

def rms_scale(row_block, gain_vector):
    inverse = lax.rsqrt(lax.optimization_barrier(jnp.mean(row_block * row_block, axis=-1, keepdims=True)) + norm_epsilon)
    return row_block * inverse * gain_vector

def attend_group(query_group, key_group, value_group, bias_block):
    scores = jnp.einsum('gqhe,gkhe->ghqk', query_group, key_group, precision=highest)
    scores = low_back(scores + bias_block[None])
    attention_weights = jax.nn.softmax(scores, axis=-1)
    context = jnp.einsum('ghqk,gkhe->gqhe', low(attention_weights), value_group, precision=highest)
    return both_ways(context)

def expert_branch(routed_pad, weight_in, weight_out, chosen):
    hidden = low_back(jnp.dot(routed_pad[chosen], weight_in, precision=highest))
    activated = low(jax.nn.gelu(hidden, approximate=True))
    return both_ways(jnp.dot(activated, weight_out, precision=highest))

def forward(tokens_wide, query_weight, key_weight, value_weight, output_weight, gain_one, gain_two, router_weight, table_wide, expert_in_wide, expert_out_wide, routes, chosen_all, bucket_of):
    token_total = tokens_wide.shape[0]
    model_width = tokens_wide.shape[1]
    head_count = table_wide.shape[1]
    head_size = model_width // head_count
    positions = jnp.arange(LEN, dtype=jnp.int32)
    relative = positions[None, :] - positions[:, None] + (LEN - 1)
    per_offset = table_wide[bucket_of]
    bias_block = jnp.transpose(per_offset[relative], (2, 0, 1))
    normed_one = low(rms_scale(tokens_wide, gain_one))
    query_rows = both_ways(jnp.dot(normed_one, query_weight, precision=highest))
    key_rows = both_ways(jnp.dot(normed_one, key_weight, precision=highest))
    value_rows = both_ways(jnp.dot(normed_one, value_weight, precision=highest))
    group_size = math.gcd(token_total // LEN, max(1, 4096 // LEN))
    group_shape = (token_total // (group_size * LEN), group_size, LEN, head_count, head_size)

    def attend_step(grouped):
        return attend_group(grouped[0], grouped[1], grouped[2], bias_block)
    context = lax.map(jax.checkpoint(attend_step), (query_rows.reshape(group_shape), key_rows.reshape(group_shape), value_rows.reshape(group_shape)))
    context = context.reshape(token_total, model_width)
    attended = low_back(jnp.dot(context, output_weight, precision=highest))
    middle = tokens_wide + attended
    normed_two = low(rms_scale(middle, gain_two))
    logits = low_back(jnp.dot(normed_two, router_weight, precision=highest))
    router_probs = jax.nn.softmax(logits, axis=-1)
    gate_value = jnp.take_along_axis(router_probs, routes[:, None], axis=1)[:, 0]
    routed = low_back(normed_two)
    routed_pad = jnp.concatenate([routed, jnp.zeros((1, model_width), jnp.float32)], axis=0)

    def expert_step(stacked):
        return expert_branch(routed_pad, stacked[0], stacked[1], stacked[2])
    produced = lax.map(jax.checkpoint(expert_step), (expert_in_wide, expert_out_wide, chosen_all))
    expert_rows = jnp.zeros((token_total + 1, model_width), jnp.float32).at[chosen_all.reshape(-1)].add(produced.reshape(-1, model_width))[:token_total]
    return middle + gate_value[:, None] * expert_rows

def reference(tokens, w_query, w_key, w_value, w_output, norm1_gain, norm2_gain, router, bias_table, expert_in, expert_out, routes, bucket_of, cotangent):
    token_total = tokens.shape[0]
    most_rows = N_SHARD * N_REP * CAP
    expert_ids = jnp.arange(router.shape[1], dtype=jnp.int32)

    def rows_of(expert_id):
        return jnp.nonzero(routes == expert_id, size=most_rows, fill_value=token_total)[0].astype(jnp.int32)
    chosen_all = lax.map(rows_of, expert_ids)
    floats = tuple((argument.astype(jnp.float32) for argument in (tokens, w_query, w_key, w_value, w_output, norm1_gain, norm2_gain, router, bias_table, expert_in, expert_out)))

    def closed(*weights):
        return forward(*weights, routes, chosen_all, bucket_of)
    output_wide, pullback = jax.vjp(closed, *floats)
    gradients = pullback(cotangent.astype(jnp.float32))
    return (output_wide.astype(jnp.bfloat16), gradients[0].astype(jnp.bfloat16), gradients[1], gradients[2], gradients[3], gradients[4], gradients[5], gradients[6], gradients[7], gradients[8], gradients[9], gradients[10])
```

```python
import functools

import jax
import jax.numpy as jnp
from jax import lax
from jax.experimental import pallas as pl
from jax.experimental.pallas import tpu as pltpu
from jax.sharding import PartitionSpec as P

LEN = 512
SPAN = 2 * LEN
HEAD = 64
PAIR = 2 * HEAD
MISC = 128
ROW_CHUNK = 4096
FF_BLOCK = 256

norm_epsilon = 1e-06
bf16 = jnp.bfloat16
f32 = jnp.float32


def dot_nt(left, right):
    return lax.dot_general(left, right, (((1,), (1,)), ((), ())), preferred_element_type=f32)


def dot_nn(left, right):
    return lax.dot_general(left, right, (((1,), (0,)), ((), ())), preferred_element_type=f32)


def dot_tn(left, right):
    return lax.dot_general(left, right, (((0,), (0,)), ((), ())), preferred_element_type=f32)


def attend_forward_kernel(query_ref, key_ref, value_ref, offset_ref, context_ref, probs_ref):
    for head in range(2):
        columns = slice(head * HEAD, (head + 1) * HEAD)
        row = jnp.broadcast_to(offset_ref[0, head : head + 1, :], (LEN, SPAN))
        bias = pltpu.roll(row, LEN + 1, axis=1, stride=1, stride_axis=0)[:, :LEN]
        scores = dot_nt(query_ref[:, columns], key_ref[:, columns]) + bias
        weights = jnp.exp(scores - jnp.max(scores, axis=-1, keepdims=True))
        probs = weights / jnp.sum(weights, axis=-1, keepdims=True)
        probs_low = probs.astype(bf16)
        probs_ref[head] = probs_low
        context_ref[:, columns] = dot_nn(probs_low, value_ref[:, columns]).astype(bf16)


def attend_backward_kernel(
    query_ref, key_ref, value_ref, grad_ref, probs_ref, grads_ref, offset_ref
):
    rows = lax.broadcasted_iota(jnp.int32, (LEN, LEN), 0)
    cols = lax.broadcasted_iota(jnp.int32, (LEN, LEN), 1)
    flip = jnp.where(rows + cols == LEN - 1, 1.0, 0.0).astype(bf16)
    for head in range(2):
        columns = slice(head * HEAD, (head + 1) * HEAD)
        grad = grad_ref[:, columns]
        probs_low = probs_ref[head]
        probs = probs_low.astype(f32)
        grad_probs = dot_nt(grad, value_ref[:, columns])
        inner = jnp.sum(probs * grad_probs, axis=-1, keepdims=True)
        grad_scores = (probs * (grad_probs - inner)).astype(bf16)
        grads_ref[0, :, columns] = dot_nn(grad_scores, key_ref[:, columns]).astype(bf16)
        grads_ref[1, :, columns] = dot_tn(grad_scores, query_ref[:, columns]).astype(bf16)
        grads_ref[2, :, columns] = dot_tn(probs_low, grad).astype(bf16)
        flipped = dot_nn(flip, grad_scores)
        wide = jnp.concatenate([flipped, jnp.zeros((LEN, SPAN - LEN), f32)], axis=1)
        skewed = pltpu.roll(wide, 0, axis=1, stride=1, stride_axis=0)
        offset_ref[0, 0, head : head + 1, :] = jnp.sum(skewed, axis=0, keepdims=True)


def attend_forward(qkv, offset_rows, seq_count, pair_count):
    width = pair_count * PAIR

    def part(at):
        return pl.BlockSpec((LEN, PAIR), lambda s, p: (s, at * pair_count + p))

    return pl.pallas_call(
        attend_forward_kernel,
        grid=(seq_count, pair_count),
        in_specs=[
            part(0),
            part(1),
            part(2),
            pl.BlockSpec((1, 2, SPAN), lambda s, p: (p, 0, 0)),
        ],
        out_specs=[
            pl.BlockSpec((LEN, PAIR), lambda s, p: (s, p)),
            pl.BlockSpec((2, LEN, LEN), lambda s, p: (s * pair_count + p, 0, 0)),
        ],
        out_shape=[
            jax.ShapeDtypeStruct((seq_count * LEN, width), bf16),
            jax.ShapeDtypeStruct((seq_count * pair_count * 2, LEN, LEN), bf16),
        ],
        compiler_params=pltpu.CompilerParams(vmem_limit_bytes=48 * 1024 * 1024),
    )(qkv, qkv, qkv, offset_rows)


def attend_backward(qkv, grad_context, probs, seq_count, pair_count):
    width = pair_count * PAIR

    def part(at):
        return pl.BlockSpec((LEN, PAIR), lambda s, p: (s, at * pair_count + p))

    return pl.pallas_call(
        attend_backward_kernel,
        grid=(seq_count, pair_count),
        in_specs=[
            part(0),
            part(1),
            part(2),
            pl.BlockSpec((LEN, PAIR), lambda s, p: (s, p)),
            pl.BlockSpec((2, LEN, LEN), lambda s, p: (s * pair_count + p, 0, 0)),
        ],
        out_specs=[
            pl.BlockSpec((3, LEN, PAIR), lambda s, p: (0, s, p)),
            pl.BlockSpec((1, 1, 2, SPAN), lambda s, p: (s, p, 0, 0)),
        ],
        out_shape=[
            jax.ShapeDtypeStruct((3, seq_count * LEN, width), bf16),
            jax.ShapeDtypeStruct((seq_count, pair_count, 2, SPAN), f32),
        ],
        compiler_params=pltpu.CompilerParams(vmem_limit_bytes=48 * 1024 * 1024),
    )(qkv, qkv, qkv, grad_context, probs)


def gelu_pair(values):
    square = values * values
    bent = jnp.tanh(0.7978845608 * (values + 0.044715 * square * values))
    half = 0.5 + 0.5 * bent
    slope = half + 0.5 * values * (1.0 - bent * bent) * (
        0.7978845608 + 0.7978845608 * 3.0 * 0.044715 * square
    )
    return values * half, slope


def expert_grads_kernel(piece, rows_ref, grads_ref, in_ref, out_ref, grad_in_ref, grad_out_ref):
    chunk = pl.program_id(1)
    weight_in = in_ref[...].T
    weight_out = out_ref[...]
    total_in = None
    total_out = None
    for start in range(0, rows_ref.shape[0], piece):
        rows = rows_ref[start : start + piece, :]
        grads = grads_ref[start : start + piece, :]
        activated, slope = gelu_pair(dot_nt(weight_in, rows))
        grad_hidden = (dot_nt(weight_out, grads) * slope).astype(bf16)
        step_out = dot_nn(activated.astype(bf16), grads)
        step_in = dot_nn(grad_hidden, rows)
        total_in = step_in if total_in is None else total_in + step_in
        total_out = step_out if total_out is None else total_out + step_out

    @pl.when(chunk == 0)
    def _():
        grad_in_ref[...] = total_in.T
        grad_out_ref[...] = total_out

    @pl.when(chunk > 0)
    def _():
        grad_in_ref[...] += total_in.T
        grad_out_ref[...] += total_out


def expert_grads(rows, grads, weight_in, weight_out):
    row_count, width = rows.shape
    hidden = weight_in.shape[1]
    chunk = min(ROW_CHUNK, row_count)
    return pl.pallas_call(
        functools.partial(expert_grads_kernel, min(1024, chunk)),
        grid=(hidden // FF_BLOCK, row_count // chunk),
        in_specs=[
            pl.BlockSpec((chunk, width), lambda f, c: (c, 0)),
            pl.BlockSpec((chunk, width), lambda f, c: (c, 0)),
            pl.BlockSpec((width, FF_BLOCK), lambda f, c: (0, f)),
            pl.BlockSpec((FF_BLOCK, width), lambda f, c: (f, 0)),
        ],
        out_specs=[
            pl.BlockSpec((width, FF_BLOCK), lambda f, c: (0, f)),
            pl.BlockSpec((FF_BLOCK, width), lambda f, c: (f, 0)),
        ],
        out_shape=[
            jax.ShapeDtypeStruct((width, hidden), f32),
            jax.ShapeDtypeStruct((hidden, width), f32),
        ],
        compiler_params=pltpu.CompilerParams(vmem_limit_bytes=56 * 1024 * 1024),
        cost_estimate=pl.CostEstimate(
            flops=8 * row_count * width * hidden,
            bytes_accessed=4 * row_count * width + 12 * width * hidden,
            transcendentals=row_count * hidden,
        ),
    )(rows, grads, weight_in, weight_out)


def scatter_sum(packed, shard_count):
    rows = packed.shape[0] // shard_count
    parts = packed.reshape(shard_count, rows, packed.shape[1])
    parts = lax.all_to_all(parts, "shard", split_axis=0, concat_axis=0, tiled=True)
    return jnp.sum(parts.astype(f32), axis=0)


def body(
    tokens,
    w_query,
    w_key,
    w_value,
    w_output,
    norm1_gain,
    norm2_gain,
    router,
    bias_table,
    expert_in,
    expert_out,
    routes,
    bucket_of,
    cotangent,
):
    shard_count = lax.axis_size("shard")
    own_rows = w_query.shape[0]
    width = w_query.shape[1]
    table_rows, head_count = bias_table.shape
    bucket_count = table_rows * shard_count
    expert_count = router.shape[1]
    pair_count = head_count // 2
    token_count = tokens.shape[0]
    seq_count = token_count // LEN
    capacity = 2 * token_count // shard_count
    slot_count = expert_count * capacity

    misc = jnp.concatenate(
        [
            router,
            norm1_gain[:, None],
            norm2_gain[:, None],
            jnp.pad(bias_table, ((0, own_rows - table_rows), (0, 0))),
        ],
        axis=1,
    )
    misc = jnp.pad(misc, ((0, 0), (0, MISC - misc.shape[1])))
    first = lax.all_gather(
        jnp.concatenate([w_query, w_key, w_value, misc], axis=1), "shard", axis=0, tiled=True
    )
    output_full = lax.all_gather(w_output, "shard", axis=0, tiled=True)
    qkv_full = first[:, : 3 * width]
    misc_full = first[:, 3 * width :]
    router_full = misc_full[:, :expert_count]
    gain_one = misc_full[:, expert_count].astype(f32)
    gain_two = misc_full[:, expert_count + 1].astype(f32)
    table_at = expert_count + 2
    table_full = misc_full.reshape(shard_count, own_rows, MISC)[
        :, :table_rows, table_at : table_at + head_count
    ].reshape(bucket_count, head_count)

    route_onehot = routes[:, None] == jnp.arange(expert_count, dtype=jnp.int32)[None, :]
    route_mask = route_onehot.astype(f32)
    route_counts = route_onehot.astype(jnp.int32)
    earlier = jnp.cumsum(route_counts, axis=0) - route_counts
    rank_value = jnp.sum(earlier * route_counts, axis=-1)
    slot_index = routes * capacity + rank_value
    select = (
        jnp.arange(slot_count, dtype=jnp.int32)[:, None] == slot_index[None, :]
    ).astype(bf16)

    bucket_onehot = (
        bucket_of[:, None] == jnp.arange(bucket_count, dtype=jnp.int32)[None, :]
    ).astype(f32)
    bucket_onehot = jnp.pad(bucket_onehot, ((0, SPAN - bucket_onehot.shape[0]), (0, 0)))
    offset_rows = jnp.dot(
        table_full.astype(f32).T, bucket_onehot.T, precision=lax.Precision.HIGHEST
    ).reshape(pair_count, 2, SPAN)

    tokens_wide = tokens.astype(f32)
    first_scale = lax.rsqrt(
        jnp.mean(tokens_wide * tokens_wide, axis=-1, keepdims=True) + norm_epsilon
    )
    normed_low = (tokens_wide * first_scale * gain_one).astype(bf16)
    qkv = jnp.dot(normed_low, qkv_full, preferred_element_type=f32).astype(bf16)
    context_rows, probs = attend_forward(qkv, offset_rows, seq_count, pair_count)
    attended = jnp.dot(context_rows, output_full, preferred_element_type=f32)
    middle = tokens_wide + attended
    second_scale = lax.rsqrt(jnp.mean(middle * middle, axis=-1, keepdims=True) + norm_epsilon)
    routed_low = (middle * second_scale * gain_two).astype(bf16)
    outgoing = jnp.dot(select, routed_low, preferred_element_type=f32).astype(bf16)
    received = lax.all_to_all(
        outgoing.reshape(expert_count, capacity, width),
        "shard",
        split_axis=0,
        concat_axis=0,
        tiled=True,
    ).reshape(slot_count, width)

    logits = jnp.dot(routed_low, router_full, preferred_element_type=f32)
    router_probs = jax.nn.softmax(logits, axis=-1)
    gate_value = jnp.sum(router_probs * route_mask, axis=-1, keepdims=True)
    grad_out = cotangent.astype(f32)
    grad_result = (gate_value * grad_out).astype(bf16)
    grad_outgoing = jnp.dot(select, grad_result, preferred_element_type=f32).astype(bf16)
    grad_received = lax.all_to_all(
        grad_outgoing.reshape(expert_count, capacity, width),
        "shard",
        split_axis=0,
        concat_axis=0,
        tiled=True,
    ).reshape(slot_count, width)

    all_received = lax.all_gather(received, "rep", axis=0, tiled=True)
    all_grads = lax.all_gather(grad_received, "rep", axis=0, tiled=True)

    weight_in = expert_in[0]
    weight_out = expert_out[0]
    hidden = jnp.dot(received, weight_in, preferred_element_type=f32)
    activated, slope = gelu_pair(hidden)
    produced = jnp.dot(activated.astype(bf16), weight_out, preferred_element_type=f32).astype(bf16)
    returned = lax.all_to_all(
        produced.reshape(expert_count, capacity, width),
        "shard",
        split_axis=0,
        concat_axis=0,
        tiled=True,
    ).reshape(slot_count, width)
    grad_activated = dot_nt(grad_received, weight_out)
    grad_hidden = (grad_activated * slope).astype(bf16)
    grad_routed = dot_nt(grad_hidden, weight_in).astype(bf16)
    grad_back = lax.all_to_all(
        grad_routed.reshape(expert_count, capacity, width),
        "shard",
        split_axis=0,
        concat_axis=0,
        tiled=True,
    ).reshape(slot_count, width)

    expert_rows = dot_tn(select, returned)
    output_rows = (middle + gate_value * expert_rows).astype(bf16)
    grad_gate = jnp.sum(grad_out * expert_rows, axis=-1, keepdims=True)
    grad_logits = (grad_gate * gate_value * (route_mask - router_probs)).astype(bf16)
    grad_router = dot_tn(routed_low, grad_logits)
    grad_normed_two = dot_nt(grad_logits, router_full) + dot_tn(select, grad_back)
    grad_gain_two = jnp.sum(grad_normed_two * middle * second_scale, axis=0)
    pulled = gain_two * grad_normed_two
    grad_middle = (
        grad_out
        + second_scale * pulled
        - middle
        * (second_scale * second_scale * second_scale)
        * jnp.mean(pulled * middle, axis=-1, keepdims=True)
    )
    grad_attended = grad_middle.astype(bf16)
    grad_output_weight = dot_tn(context_rows, grad_attended)
    grad_context = dot_nt(grad_attended, output_full).astype(bf16)
    grads, offset_grads = attend_backward(qkv, grad_context, probs, seq_count, pair_count)

    early = jnp.concatenate([grad_router, grad_gain_two[:, None]], axis=1)
    early = jnp.pad(early, ((0, 0), (0, MISC - early.shape[1]))).astype(bf16)
    early = jnp.concatenate([grad_output_weight.astype(bf16), early], axis=1)
    early_share = scatter_sum(early, shard_count)

    grad_offsets = jnp.sum(offset_grads, axis=0).reshape(head_count, SPAN)
    grad_table = jnp.dot(bucket_onehot.T, grad_offsets.T, precision=lax.Precision.HIGHEST)
    grad_normed_one = (
        dot_nt(grads[0], qkv_full[:, :width])
        + dot_nt(grads[1], qkv_full[:, width : 2 * width])
        + dot_nt(grads[2], qkv_full[:, 2 * width :])
    )
    grad_gain_one = jnp.sum(grad_normed_one * tokens_wide * first_scale, axis=0)
    table_part = jnp.pad(
        grad_table.reshape(shard_count, table_rows, head_count),
        ((0, 0), (0, own_rows - table_rows), (0, 0)),
    ).reshape(width, head_count)
    late = jnp.concatenate([grad_gain_one[:, None], table_part], axis=1)
    late = jnp.pad(late, ((0, 0), (0, MISC - late.shape[1]))).astype(bf16)
    late = jnp.concatenate(
        [dot_tn(normed_low, grads[k]).astype(bf16) for k in range(3)] + [late], axis=1
    )
    late_share = scatter_sum(late, shard_count)

    pushed = gain_one * grad_normed_one
    grad_tokens = (
        grad_middle
        + first_scale * pushed
        - tokens_wide
        * (first_scale * first_scale * first_scale)
        * jnp.mean(pushed * tokens_wide, axis=-1, keepdims=True)
    ).astype(bf16)

    summed_in, summed_out = expert_grads(all_received, all_grads, weight_in, weight_out)

    share = jnp.concatenate([early_share, late_share], axis=1).astype(bf16)
    final = jnp.sum(lax.all_gather(share, "rep", axis=0, tiled=False).astype(f32), axis=0)
    final_early = final[:, width : width + MISC]
    final_late = final[:, 4 * width + MISC :]
    return (
        output_rows,
        grad_tokens,
        final[:, width + MISC : 2 * width + MISC],
        final[:, 2 * width + MISC : 3 * width + MISC],
        final[:, 3 * width + MISC : 4 * width + MISC],
        final[:, :width],
        final_late[:, 0],
        final_early[:, expert_count],
        final_early[:, :expert_count],
        final_late[:table_rows, 1 : 1 + head_count],
        summed_in[None],
        summed_out[None],
    )


def solution(mesh):
    placed = (
        P(("shard", "rep"), None),
        P("shard", None),
        P("shard", None),
        P("shard", None),
        P("shard", None),
        P("shard"),
        P("shard"),
        P("shard", None),
        P("shard", None),
        P("shard", None, None),
        P("shard", None, None),
        P(("shard", "rep")),
        P(),
        P(("shard", "rep"), None),
    )
    return jax.shard_map(
        body,
        mesh=mesh,
        in_specs=placed,
        out_specs=(
            P(("shard", "rep"), None),
            P(("shard", "rep"), None),
            P("shard", None),
            P("shard", None),
            P("shard", None),
            P("shard", None),
            P("shard"),
            P("shard"),
            P("shard", None),
            P("shard", None),
            P("shard", None, None),
            P("shard", None, None),
        ),
        check_vma=False,
    )
```
